32 devices in a mesh: rep: 2 (over core), dp: 4 (over y, x), expert: 4 (over z).
Axes of the slice: x: 2, y: 2, z: 4, core: 2. Of those that a mesh axis runs over, the one named last changes fastest.
Arguments:
- tokens: bfloat16 [32768, 768], P(('rep', 'dp', 'expert')), may hold values from -6 to 6
- routes: int32 [32768, 2], P(('rep', 'dp', 'expert')), may hold values from 0 to 7, all different within a row; in each aligned block of 1024 rows (0 to 1023, 1024 to 2047, ...) at most 384 rows name the same one
- cotangent: bfloat16 [32768, 768], P(('rep', 'dp', 'expert')), may hold values from -6 to 6
- w_query: bfloat16 [768, 768], P('dp'), may hold values from -0.21875 to 0.21875
- w_key: bfloat16 [768, 768], P('dp'), may hold values from -0.21875 to 0.21875
- w_value: bfloat16 [768, 768], P('dp'), may hold values from -0.21875 to 0.21875
- w_out: bfloat16 [768, 768], P('dp'), may hold values from -0.875 to 0.875
- w_router: bfloat16 [768, 8], P('dp'), may hold values from -0.15625 to 0.15625
- gain_attn: bfloat16 [768], P('dp'), may hold values from 0.099609375 to 1.8984375
- gain_moe: bfloat16 [768], P('dp'), may hold values from 0.099609375 to 1.8984375
- bias_table: bfloat16 [32, 12], P('dp'), may hold values from -4 to 4
- expert_up: bfloat16 [8, 768, 3072], P('expert', None, 'dp'), may hold values from -0.21875 to 0.21875
- expert_down: bfloat16 [8, 3072, 768], P('expert', 'dp'), may hold values from -0.21875 to 0.21875
Outputs:
- output: bfloat16 [32768, 768], P(('rep', 'dp', 'expert'))
- grad_tokens: float32 [32768, 768], P(('rep', 'dp', 'expert'))
- grad_query: float32 [768, 768], P('dp')
- grad_key: float32 [768, 768], P('dp')
- grad_value: float32 [768, 768], P('dp')
- grad_out: float32 [768, 768], P('dp')
- grad_router: float32 [768, 8], P('dp')
- grad_gain_attn: float32 [768], P('dp')
- grad_gain_moe: float32 [768], P('dp')
- grad_table: float32 [32, 12], P('dp')
- grad_up: float32 [8, 768, 3072], P('expert', None, 'dp')
- grad_down: float32 [8, 3072, 768], P('expert', 'dp')
The draws below stay inside these ranges and needn't reach their ends.
Inputs may be any that keep to these rules, and one draw needn't show every extreme that they name: `routes`: each row names 2 different experts; among the 1024 rows of one sequence no expert is named more than 384 times, a bound that some block reaches; every expert is named somewhere.
All inputs are finite; a program needn't handle non-finite values.
Results may differ from the reference program's by a relative error of at most 0.019.
Values may be sent and summed in bfloat16 or wider, within the bound.
A program may use at most 384 MiB of HBM per device.

```python
import math
import jax
import jax.numpy as jnp
import numpy as np
from jax import lax

D = 768
HEADS = 12
HD = 64
FF = 3072
TOP = 2
BUCKETS = 32
SEQ = 1024
SEQS = 32
TOKENS = 32768
EXPERTS = 8
CAP = 384
N_DP = 4


def level_of(key, dims, cuts, low, largest):
    def one(position, blocks):
        draws = jax.random.uniform(jax.random.fold_in(jax.random.fold_in(key, 6), position), (blocks,), jnp.float32, low / len(cuts), largest / len(cuts))
        return jnp.repeat(jnp.exp(draws), dims[position] // blocks).reshape((-1,) + (1,) * (len(dims) - position - 1))

    level = one(*cuts[0])
    for cut in cuts[1:]:
        level = level * one(*cut)
    return level


def shared_out(own_key, own, number, rows, amount, top, bound, slope):
    order = jax.random.permutation(own_key, amount)
    packed, ordinary = portions_of(amount, rows * top, bound, slope, True), portions_of(amount, rows * top, bound, slope, False)
    places = jnp.arange(amount)

    def named(lengths, rotation):
        used = int((lengths > 0).sum())
        fixed = max(1, used // 4)
        shifted = fixed + (places - fixed + rotation * (used - fixed)) % max(1, amount - fixed)
        return jnp.zeros((amount,), jnp.int32).at[order[jnp.where(places < fixed, places, shifted)]].set(jnp.asarray(lengths, jnp.int32))

    lengths = jnp.where(number % 4 == 0, named(packed, number // 4), named(ordinary, number - number // 4 - 1))
    mixed = jax.random.permutation(jax.random.fold_in(own, 3), amount)
    donor, receiver = mixed[0:amount // 2 * 2:2], mixed[1:amount // 2 * 2:2]
    slack = jnp.minimum(lengths[donor] - 1, bound - lengths[receiver]) // 2
    slack = jnp.where((donor == order[0]) | (receiver == order[0]) | (lengths[receiver] == 0), 0, jnp.maximum(slack, 0))
    shifted = jax.random.randint(jax.random.fold_in(own, 4), (amount // 2,), 0, 1 << 20) % (slack + 1)
    lengths = lengths.at[donor].add(-shifted).at[receiver].add(shifted)
    items = jnp.searchsorted(jnp.cumsum(lengths), jnp.arange(rows * top), side="right").astype(jnp.int32)
    table = items.reshape(top, rows).T
    table = table[jax.random.permutation(jax.random.fold_in(own, 1), rows)]
    rotation = jax.random.randint(jax.random.fold_in(own, 2), (rows, 1), 0, top)
    return jnp.take_along_axis(table, (jnp.arange(top)[None, :] + rotation) % top, axis=1)


def portions_of(count, total, reach, skew, full):
    loads = [(1 << 20) // math.isqrt(grade ** skew) + 1 for grade in range(1, count + 1)]
    largest = reach if full else min(reach, max(-(-total // count), total * loads[0] // sum(loads)))
    least = 1 if total - largest >= count - 1 else 0
    holding, spare = [largest] + [least] * (count - 1), total - largest - least * (count - 1)
    while spare > 0:
        candidates = [i for i in range(1, count) if holding[i] < largest] or [i for i in range(1, count) if holding[i] < reach]
        whole, left = sum([loads[i] for i in candidates]), spare
        for i in candidates:
            extra = min(reach - holding[i], max(1, left * loads[i] // whole), spare)
            holding[i] = holding[i] + extra
            spare = spare - extra
    return np.array(holding)


def bell_draw(key, extent, spread, bound, cuts=(), held_as=jnp.bfloat16):
    values = spread * jax.random.normal(key, extent, jnp.float32)
    if cuts:
        values = values * level_of(key, extent, cuts, -0.22, 0.18)
    return jnp.clip(values, -bound, bound).astype(held_as)


def setup_inputs(seed: int = 0) -> dict:
    splits = jax.random.split(jax.random.key(seed), 14)
    tokens = bell_draw(splits[0], (TOKENS, D), 1.0, 6.0, ((0, 32),))
    routes_keys = jax.random.split(jax.random.fold_in(splits[1], 1), TOKENS // SEQ)
    routes_turns = jax.random.permutation(jax.random.fold_in(splits[1], 3), TOKENS // SEQ)
    routes = jax.vmap(lambda own, number: shared_out(jax.random.fold_in(splits[1], 2), own, number, SEQ, EXPERTS, TOP, CAP, 1))(routes_keys, routes_turns).reshape((TOKENS, TOP))
    cotangent = bell_draw(splits[2], (TOKENS, D), 1.0, 6.0, ((0, 32),))
    w_query = bell_draw(splits[3], (D, D), D ** -0.5, 0.21875, ((0, 4),))
    w_key = bell_draw(splits[4], (D, D), D ** -0.5, 0.21875, ((0, 4),))
    w_value = bell_draw(splits[5], (D, D), D ** -0.5, 0.21875, ((0, 4),))
    w_out = bell_draw(splits[6], (D, D), (D // 16) ** -0.5, 0.875, ((0, 4),))
    w_router = bell_draw(splits[7], (D, EXPERTS), (2 * D) ** -0.5, 0.15625, ((0, 4),))
    gain_attn = jnp.clip(1.0 + 0.18 * jax.random.normal(splits[8], (D,), jnp.float32), 0.099609375, 1.8984375).astype(jnp.bfloat16)
    gain_moe = jnp.clip(1.0 + 0.18 * jax.random.normal(splits[9], (D,), jnp.float32), 0.099609375, 1.8984375).astype(jnp.bfloat16)
    bias_table = bell_draw(splits[10], (BUCKETS, HEADS), 1.0, 4.0, ((0, 4),))
    expert_up = bell_draw(splits[11], (EXPERTS, D, FF), D ** -0.5, 0.21875, ((0, 4), (2, 4)))
    expert_down = bell_draw(splits[12], (EXPERTS, FF, D), (FF // 4) ** -0.5, 0.21875, ((0, 4), (1, 4)))
    return dict(tokens=tokens, routes=routes, cotangent=cotangent, w_query=w_query, w_key=w_key, w_value=w_value, w_out=w_out, w_router=w_router, gain_attn=gain_attn, gain_moe=gain_moe, bias_table=bias_table, expert_up=expert_up, expert_down=expert_down)


@jax.custom_vjp
def low(v):
    return lax.optimization_barrier(v.astype(jnp.bfloat16)).astype(jnp.float32)

@jax.custom_vjp
def low_back(v):
    return v

def low_keep(v):
    return (low(v), None)

def low_pass(kept, grad):
    return (grad,)

def back_keep(v):
    return (v, None)

def back_low(kept, grad):
    return (low(grad),)
low.defvjp(low_keep, low_pass)
low_back.defvjp(back_keep, back_low)
distance_edges = (18, 21, 24, 27, 31, 35, 40, 45, 51, 58, 66, 75, 85, 97, 110)

def bucket_ids(distance):
    distance = jnp.maximum(distance, 0)
    result = jnp.minimum(distance, 16)
    for edge_value in distance_edges:
        result = result + (distance >= edge_value).astype(jnp.int32)
    return result

def rms_apply(values, gain_vec):
    return values * lax.rsqrt(lax.optimization_barrier(jnp.mean(values * values, axis=-1, keepdims=True)) + 1e-06) * gain_vec

def slot_targets(route_rows, expert_count, capacity):
    flat_routes = route_rows.reshape(-1)
    one_hot = (flat_routes[:, None] == jnp.arange(expert_count, dtype=jnp.int32)[None, :]).astype(jnp.int32)
    earlier = jnp.cumsum(one_hot, axis=0) - one_hot
    return (flat_routes * capacity + lax.optimization_barrier(jnp.sum(earlier * one_hot, axis=1))).astype(jnp.int32)

def slot_sources(targets, slot_count):
    pick_ids = jnp.arange(targets.shape[0], dtype=jnp.int32)
    source_ids = jnp.zeros((slot_count,), jnp.int32).at[targets].set(pick_ids)
    occupied = jnp.zeros((slot_count,), jnp.int32).at[targets].set(1)
    return (source_ids, occupied)

def attend_one(inputs, query_w, key_w, value_w, out_w, gain_vec, table):
    highest = lax.Precision.HIGHEST
    norm_one = low(rms_apply(inputs, gain_vec))
    queries = low(low_back(jnp.dot(norm_one, query_w, precision=highest))).reshape(SEQ, HEADS, HD)
    key_rows = low(low_back(jnp.dot(norm_one, key_w, precision=highest))).reshape(SEQ, HEADS, HD)
    value_rows = low(low_back(jnp.dot(norm_one, value_w, precision=highest))).reshape(SEQ, HEADS, HD)
    positions = jnp.arange(SEQ, dtype=jnp.int32)
    distance = positions[:, None] - positions[None, :]
    position_bias = jnp.transpose(table[bucket_ids(distance)], (2, 0, 1))
    scores = jnp.einsum('ihd,jhd->hij', queries, key_rows, precision=highest) * HD ** (-0.5) + position_bias
    scores = low_back(scores)
    scores = jnp.where((distance >= 0)[None], scores, -1e+30)
    probs = low(jax.nn.softmax(scores, axis=-1))
    heads_out = jnp.einsum('hij,jhd->ihd', probs, value_rows, precision=highest).reshape(SEQ, D)
    heads_out = low(low_back(heads_out))
    return inputs + low_back(jnp.dot(heads_out, out_w, precision=highest))

def reference(tokens, routes, cotangent, w_query, w_key, w_value, w_out, w_router, gain_attn, gain_moe, bias_table, expert_up, expert_down):
    highest = lax.Precision.HIGHEST
    params = tuple((array.astype(jnp.float32) for array in (tokens, w_query, w_key, w_value, w_out, w_router, gain_attn, gain_moe, bias_table, expert_up, expert_down)))
    route_seq = routes.reshape(SEQS, SEQ, TOP)
    targets = jax.vmap(lambda route_rows: slot_targets(route_rows, EXPERTS, CAP))(route_seq)
    source_ids, occupied = jax.vmap(lambda target_rows: slot_sources(target_rows, EXPERTS * CAP))(targets)
    quarter = FF // N_DP

    def forward(inputs, query_w, key_w, value_w, out_w, router_w, gain_one, gain_two, table, up_all, down_all):

        def one_seq(seq_in):
            return attend_one(seq_in, query_w, key_w, value_w, out_w, gain_one, table)
        middle = lax.map(jax.checkpoint(one_seq), inputs.reshape(SEQS, SEQ, D))
        norm_two = low(rms_apply(middle, gain_two))
        logits = jnp.einsum('std,de->ste', norm_two, router_w, precision=highest)
        gate_vals = jax.nn.softmax(jnp.take_along_axis(logits, route_seq, axis=2), axis=-1)
        gathered = jnp.take_along_axis(norm_two, (source_ids // TOP)[:, :, None], axis=1)
        dispatched = jnp.where(occupied[:, :, None] > 0, gathered, 0.0)
        dispatched = jnp.transpose(dispatched.reshape(SEQS, EXPERTS, CAP, D), (1, 0, 2, 3)).reshape(EXPERTS, SEQS * CAP, D)
        dispatched = low_back(dispatched)

        def one_expert(pieces):
            rows_in, up_one, down_one = pieces
            total = jnp.zeros((rows_in.shape[0], D), jnp.float32)
            for part_index in range(N_DP):
                rows_part = low_back(rows_in)
                up_part = up_one[:, part_index * quarter:(part_index + 1) * quarter]
                down_part = down_one[part_index * quarter:(part_index + 1) * quarter]
                pre_act = low_back(jnp.dot(rows_part, up_part, precision=highest))
                hidden = low(jax.nn.gelu(pre_act, approximate=False))
                total = total + low(jnp.dot(hidden, down_part, precision=highest))
            return low(low_back(total))
        expert_out = lax.map(jax.checkpoint(one_expert), (dispatched, up_all, down_all))
        returned = jnp.transpose(expert_out.reshape(EXPERTS, SEQS, CAP, D), (1, 0, 2, 3)).reshape(SEQS, EXPERTS * CAP, D)
        picked = jnp.take_along_axis(returned, targets[:, :, None], axis=1).reshape(SEQS, SEQ, TOP, D)
        moe_out = lax.optimization_barrier(jnp.sum(gate_vals[..., None] * picked, axis=2))
        return (middle + moe_out).reshape(TOKENS, D)
    output, pull = jax.vjp(forward, *params)
    grads = pull(cotangent.astype(jnp.float32))
    return (output.astype(jnp.bfloat16), grads[0], grads[1], grads[2], grads[3], grads[4], grads[5], grads[6], grads[7], grads[8], grads[9], grads[10])
```

```python
import jax
import jax.numpy as jnp
from jax import lax
from jax.experimental import pallas as pl
from jax.experimental.pallas import tpu as pltpu
from jax.sharding import PartitionSpec as P

distance_edges = (18, 21, 24, 27, 31, 35, 40, 45, 51, 58, 66, 75, 85, 97, 110)


def bucket_ids(distance):
    distance = jnp.maximum(distance, 0)
    result = jnp.minimum(distance, 16)
    for edge_value in distance_edges:
        result = result + (distance >= edge_value).astype(jnp.int32)
    return result


def dot_f32(left, right, left_dim, right_dim):
    return lax.dot_general(
        left, right, (((left_dim,), (right_dim,)), ((), ())), preferred_element_type=jnp.float32
    )


TILE = 128
QUERY_ROWS = 256
HEAD_DIM = 64


def key_segments(begin):
    near_begin = max(begin - TILE, 0)
    parts = [(near_begin, begin + QUERY_ROWS, near_begin - (begin - TILE))]
    if near_begin > 0:
        parts.append((0, near_begin, None))
    return parts


def attend_kernel(q_ref, k_ref, v_ref, window_ref, out_ref, lse_ref):
    scale = HEAD_DIM ** (-0.5)
    for head in range(2):
        cols = slice(head * HEAD_DIM, (head + 1) * HEAD_DIM)
        for begin in range(0, q_ref.shape[0], QUERY_ROWS):
            rows = slice(begin, begin + QUERY_ROWS)
            query = (q_ref[rows, cols].astype(jnp.float32) * scale).astype(jnp.bfloat16)
            parts = key_segments(begin)
            scores = []
            for low, high, window_row in parts:
                score = dot_f32(k_ref[low:high, cols], query, 1, 1)
                if window_row is not None:
                    score = score + window_ref[head, window_row:, :]
                scores.append(score)
            row_max = jnp.max(scores[0], axis=0, keepdims=True)
            for score in scores[1:]:
                row_max = jnp.maximum(row_max, jnp.max(score, axis=0, keepdims=True))
            total = jnp.zeros((1, QUERY_ROWS), jnp.float32)
            acc = jnp.zeros((HEAD_DIM, QUERY_ROWS), jnp.float32)
            for (low, high, window_row), score in zip(parts, scores):
                prob = jnp.exp(score - row_max)
                total = total + jnp.sum(prob, axis=0, keepdims=True)
                acc = acc + dot_f32(v_ref[low:high, cols], prob.astype(jnp.bfloat16), 0, 0)
            out_ref[rows, cols] = (acc / total).T.astype(jnp.bfloat16)
            lse_ref[0, head : head + 1, rows] = row_max + jnp.log(total)


def attend_grad_kernel(
    q_ref, k_ref, v_ref, go_ref, window_ref, lse_ref, dq_ref, dk_ref, dv_ref, tile_ref, dk_acc, dv_acc
):
    scale = HEAD_DIM ** (-0.5)
    first = slice(0, TILE)
    second = slice(TILE, 2 * TILE)
    for head in range(2):
        cols = slice(head * HEAD_DIM, (head + 1) * HEAD_DIM)
        tile_ref[head] = jnp.zeros((3 * TILE, TILE), jnp.float32)
        last_begin = q_ref.shape[0] - QUERY_ROWS
        for begin in range(last_begin, -1, -QUERY_ROWS):
            rows = slice(begin, begin + QUERY_ROWS)
            query = (q_ref[rows, cols].astype(jnp.float32) * scale).astype(jnp.bfloat16)
            grad_out = go_ref[rows, cols]
            lse = lse_ref[0, head : head + 1, rows]
            parts = key_segments(begin)
            probs = []
            grad_probs = []
            delta = jnp.zeros((1, QUERY_ROWS), jnp.float32)
            for low, high, window_row in parts:
                score = dot_f32(k_ref[low:high, cols], query, 1, 1)
                if window_row is not None:
                    score = score + window_ref[head, window_row:, :]
                prob = jnp.exp(score - lse)
                grad_prob = dot_f32(v_ref[low:high, cols], grad_out, 1, 1)
                delta = delta + jnp.sum(prob * grad_prob, axis=0, keepdims=True)
                probs.append(prob)
                grad_probs.append(grad_prob)
            grad_query = jnp.zeros((HEAD_DIM, QUERY_ROWS), jnp.float32)
            far_sum = jnp.zeros((TILE, TILE), jnp.float32)
            for (low, high, window_row), prob, grad_prob in zip(parts, probs, grad_probs):
                grad_score = prob * (grad_prob - delta)
                grad_bf = grad_score.astype(jnp.bfloat16)
                value_term = dot_f32(prob.astype(jnp.bfloat16), grad_out, 1, 0)
                key_term = dot_f32(grad_bf, query, 1, 0)
                if begin == last_begin:
                    dv_acc[low:high, :] = value_term
                    dk_acc[low:high, :] = key_term
                else:
                    dv_acc[low:high, :] += value_term
                    dk_acc[low:high, :] += key_term
                grad_query = grad_query + dot_f32(k_ref[low:high, cols], grad_bf, 0, 0)
                if window_row is None:
                    for chunk in range(0, high - low, TILE):
                        piece = grad_score[chunk : chunk + TILE]
                        far_sum = far_sum + piece[:, first] + piece[:, second]
                else:
                    at = TILE - window_row
                    if window_row == 0:
                        tile_ref[head, 0:TILE, :] += grad_score[0:TILE, first]
                        far_sum = far_sum + grad_score[0:TILE, second]
                    tile_ref[head, 0:TILE, :] += grad_score[at : at + TILE, second]
                    tile_ref[head, TILE : 2 * TILE, :] += (
                        grad_score[at : at + TILE, first]
                        + grad_score[at + TILE : at + 2 * TILE, second]
                    )
            tile_ref[head, 2 * TILE :, :] += far_sum
            dq_ref[rows, cols] = (grad_query * scale).T.astype(jnp.bfloat16)
        dk_ref[:, cols] = dk_acc[...].astype(jnp.bfloat16)
        dv_ref[:, cols] = dv_acc[...].astype(jnp.bfloat16)


def attend(qkv, window):
    seq_len, width = qkv.shape[0], qkv.shape[1] // 3
    pairs = width // (2 * HEAD_DIM)
    wide = (seq_len, 2 * HEAD_DIM)
    return pl.pallas_call(
        attend_kernel,
        grid=(pairs,),
        in_specs=[
            pl.BlockSpec(wide, lambda p: (0, p)),
            pl.BlockSpec(wide, lambda p: (0, p + pairs)),
            pl.BlockSpec(wide, lambda p: (0, p + 2 * pairs)),
            pl.BlockSpec((2,) + window.shape[1:], lambda p: (p, 0, 0)),
        ],
        out_specs=[
            pl.BlockSpec(wide, lambda p: (0, p)),
            pl.BlockSpec((1, 2, seq_len), lambda p: (p, 0, 0)),
        ],
        out_shape=[
            jax.ShapeDtypeStruct((seq_len, width), jnp.bfloat16),
            jax.ShapeDtypeStruct((pairs, 2, seq_len), jnp.float32),
        ],
        compiler_params=pltpu.CompilerParams(vmem_limit_bytes=48 * 1024 * 1024),
    )(qkv, qkv, qkv, window)


def attend_grad(qkv, grad_heads, window, lse):
    seq_len, width = grad_heads.shape
    pairs = width // (2 * HEAD_DIM)
    wide = (seq_len, 2 * HEAD_DIM)
    grad_shape = jax.ShapeDtypeStruct((seq_len, width), jnp.bfloat16)
    return pl.pallas_call(
        attend_grad_kernel,
        grid=(pairs,),
        in_specs=[
            pl.BlockSpec(wide, lambda p: (0, p)),
            pl.BlockSpec(wide, lambda p: (0, p + pairs)),
            pl.BlockSpec(wide, lambda p: (0, p + 2 * pairs)),
            pl.BlockSpec(wide, lambda p: (0, p)),
            pl.BlockSpec((2,) + window.shape[1:], lambda p: (p, 0, 0)),
            pl.BlockSpec((1, 2, seq_len), lambda p: (p, 0, 0)),
        ],
        out_specs=[
            pl.BlockSpec(wide, lambda p: (0, p)),
            pl.BlockSpec(wide, lambda p: (0, p)),
            pl.BlockSpec(wide, lambda p: (0, p)),
            pl.BlockSpec((2, 3 * TILE, TILE), lambda p: (p, 0, 0)),
        ],
        out_shape=[
            grad_shape,
            grad_shape,
            grad_shape,
            jax.ShapeDtypeStruct((2 * pairs, 3 * TILE, TILE), jnp.float32),
        ],
        scratch_shapes=[
            pltpu.VMEM((seq_len, HEAD_DIM), jnp.float32),
            pltpu.VMEM((seq_len, HEAD_DIM), jnp.float32),
        ],
        compiler_params=pltpu.CompilerParams(vmem_limit_bytes=48 * 1024 * 1024),
    )(qkv, qkv, qkv, grad_heads, window, lse)


def up_kernel(rows_ref, up_ref, hidden_ref, slope_ref):
    pre = dot_f32(rows_ref[0], up_ref[0], 1, 0)
    bell = jnp.exp(pre * pre * -0.5)
    inv = 1.0 / (1.0 + 0.23164189 * jnp.abs(pre))
    series = inv * (
        0.127414796
        + inv * (-0.142248368 + inv * (0.7107068705 + inv * (-0.7265760135 + inv * 0.5307027145)))
    )
    tail = series * bell
    cdf = jnp.where(pre >= 0, 1.0 - tail, tail)
    hidden_ref[0] = (pre * cdf).astype(jnp.bfloat16)
    slope_ref[0] = (cdf + pre * bell * 0.3989422804).astype(jnp.bfloat16)


def up_project(rows_in, up_full):
    experts, row_count, width = rows_in.shape
    hidden_width = up_full.shape[2]
    row_block = 512 if row_count % 512 == 0 else row_count
    col_block = 512
    shape = jax.ShapeDtypeStruct((experts, row_count, hidden_width), jnp.bfloat16)
    out_spec = pl.BlockSpec((1, row_block, col_block), lambda e, f, r: (e, r, f))
    return pl.pallas_call(
        up_kernel,
        grid=(experts, hidden_width // col_block, row_count // row_block),
        in_specs=[
            pl.BlockSpec((1, row_block, width), lambda e, f, r: (e, r, 0)),
            pl.BlockSpec((1, width, col_block), lambda e, f, r: (e, 0, f)),
        ],
        out_specs=[out_spec, out_spec],
        out_shape=[shape, shape],
        compiler_params=pltpu.CompilerParams(vmem_limit_bytes=48 * 1024 * 1024),
    )(rows_in, up_full)


def inv_rms(values):
    return lax.rsqrt(jnp.mean(values * values, axis=-1, keepdims=True) + 1e-06)


def rms_pull(values, inv, gain_vec, grad):
    normed = values * inv
    scaled = grad * gain_vec
    grad_in = inv * (scaled - normed * jnp.mean(scaled * normed, axis=-1, keepdims=True))
    return grad_in, jnp.sum(grad * normed, axis=0)


def to_experts(slots, groups):
    shape = slots.shape
    sent = slots.reshape((groups, shape[0] // groups) + shape[1:])
    got = lax.all_to_all(sent, "expert", split_axis=0, concat_axis=2, tiled=True)
    return got.reshape((got.shape[1],) + got.shape[2:])


def to_tokens(slots, groups):
    shape = slots.shape
    sent = slots.reshape((shape[0], groups, shape[1] // groups) + shape[2:])
    got = lax.all_to_all(sent, "expert", split_axis=1, concat_axis=0, tiled=True)
    return got.reshape((got.shape[0],) + got.shape[2:])


def local(
    tokens,
    routes,
    cotangent,
    w_query,
    w_key,
    w_value,
    w_out,
    w_router,
    gain_attn,
    gain_moe,
    bias_table,
    expert_up,
    expert_down,
):
    seq_len, width = tokens.shape
    head_count = bias_table.shape[1]
    local_experts = expert_up.shape[0]
    groups = lax.axis_size("expert")
    quarters = lax.axis_size("dp")
    expert_count = groups * local_experts
    top_count = routes.shape[1]
    capacity = 3 * seq_len * top_count // (2 * expert_count)
    share = w_query.shape[0]
    bias_size = bias_table.size
    small = jnp.concatenate(
        [
            w_router,
            gain_attn[:, None],
            gain_moe[:, None],
            jnp.pad(bias_table.reshape(-1), (0, share - bias_size))[:, None],
        ],
        axis=1,
    )
    small = jnp.pad(small, ((0, 0), (0, -small.shape[1] % TILE)))
    dense = lax.all_gather(
        jnp.concatenate([w_query, w_key, w_value, w_out, small], axis=1), "dp", axis=0, tiled=True
    )
    up_full = lax.all_gather(expert_up, "dp", axis=2, tiled=True)
    down_full = lax.all_gather(expert_down, "dp", axis=1, tiled=True)
    expert_range = jnp.arange(expert_count, dtype=jnp.int32)
    chosen = routes.T[:, None, :] == expert_range[None, :, None]
    match = jnp.any(chosen, axis=0)
    row_range = jnp.arange(seq_len, dtype=jnp.int32)
    before = (row_range[:, None] < row_range[None, :]).astype(jnp.bfloat16)
    position = dot_f32(match.astype(jnp.bfloat16), before, 1, 0).astype(jnp.int32)
    position = jnp.where(match, position, -1)
    slot_range = jnp.arange(capacity, dtype=jnp.int32)
    place = (position[:, None, :] == slot_range[None, :, None]).astype(jnp.bfloat16)
    place_flat = place.reshape(expert_count * capacity, seq_len)

    def dispatch(rows):
        slots = dot_f32(place_flat, rows, 1, 0).astype(jnp.bfloat16)
        return slots.reshape(expert_count, capacity, width)

    cot_in = to_experts(dispatch(cotangent), groups)

    inputs = tokens.astype(jnp.float32)
    inv_one = inv_rms(inputs)
    qkv_w = dense[:, : 3 * width]
    out_w = dense[:, 3 * width : 4 * width]
    small_full = dense[:, 4 * width :]
    router_full = small_full[:, :expert_count]
    gain_one = small_full[:, expert_count].astype(jnp.float32)
    gain_two = small_full[:, expert_count + 1].astype(jnp.float32)
    table = small_full[:, expert_count + 2].reshape(quarters, share)[:, :bias_size]
    table = table.reshape(-1, head_count)
    buckets = table.shape[0]

    near_keys = jnp.arange(-TILE, TILE, dtype=jnp.int32)
    distance = jnp.arange(TILE, dtype=jnp.int32)[None, :] - near_keys[:, None]
    bucket_range = jnp.arange(buckets, dtype=jnp.int32)
    one_hot = bucket_ids(distance)[None] == bucket_range[:, None, None]
    near = jnp.einsum(
        "kh,krc->hrc", table, one_hot.astype(jnp.bfloat16), preferred_element_type=jnp.float32
    ) - table[-1].astype(jnp.float32)[:, None, None]
    near = jnp.where(distance[None] >= 0, near, -1e30)
    beside, diagonal = near[:, :TILE], near[:, TILE:]
    window = jnp.concatenate(
        [
            jnp.concatenate([beside, jnp.zeros_like(beside)], axis=2),
            jnp.concatenate([diagonal, beside], axis=2),
            jnp.concatenate([jnp.full_like(diagonal, -1e30), diagonal], axis=2),
        ],
        axis=1,
    )

    norm_one_bf = (inputs * inv_one * gain_one).astype(jnp.bfloat16)
    qkv = dot_f32(norm_one_bf, qkv_w, 1, 0).astype(jnp.bfloat16)
    attn_bf, lse = attend(qkv, window)
    middle = inputs + dot_f32(attn_bf, out_w, 1, 0)
    inv_two = inv_rms(middle)
    norm_two_bf = (middle * inv_two * gain_two).astype(jnp.bfloat16)
    expert_in = to_experts(dispatch(norm_two_bf), groups)

    logits = dot_f32(router_full, norm_two_bf, 0, 1)
    picked = jnp.sum(jnp.where(chosen, logits[None], 0.0), axis=1)
    gates = jax.nn.softmax(picked, axis=0)
    gate_of = jnp.sum(jnp.where(chosen, gates[:, None, :], 0.0), axis=0)
    gate_slots = jnp.sum(place.astype(jnp.float32) * gate_of[:, None, :], axis=2)
    gate_in = to_experts(gate_slots, groups)

    hidden_bf, slope_bf = up_project(expert_in, up_full)
    expert_out = jnp.einsum(
        "erf,efd->erd", hidden_bf, down_full, preferred_element_type=jnp.float32
    ).astype(jnp.bfloat16)
    cot_f32 = cot_in.astype(jnp.float32)
    grad_gate_slots = to_tokens(jnp.sum(expert_out.astype(jnp.float32) * cot_f32, axis=2), groups)
    grad_expert_out = (cot_f32 * gate_in[:, :, None]).astype(jnp.bfloat16)
    grad_hidden = jnp.einsum(
        "erd,efd->erf", grad_expert_out, down_full, preferred_element_type=jnp.float32
    )
    grad_pre = (grad_hidden * slope_bf.astype(jnp.float32)).astype(jnp.bfloat16)
    grad_expert_in = jnp.einsum(
        "erf,edf->erd", grad_pre, up_full, preferred_element_type=jnp.float32
    ).astype(jnp.bfloat16)
    grad_back = to_tokens(grad_expert_in, groups)
    grad_down = jnp.einsum(
        "erf,erd->efd", hidden_bf, grad_expert_out, preferred_element_type=jnp.float32
    ).astype(jnp.bfloat16)
    grad_up = jnp.einsum(
        "erd,erf->edf", expert_in, grad_pre, preferred_element_type=jnp.float32
    ).astype(jnp.bfloat16)
    grad_down = lax.psum(lax.psum_scatter(grad_down, "dp", scatter_dimension=1, tiled=True), "rep")
    grad_up = lax.psum(lax.psum_scatter(grad_up, "dp", scatter_dimension=2, tiled=True), "rep")

    expert_out, grad_back = lax.optimization_barrier((expert_out, grad_back))
    returned = to_tokens(expert_out, groups).reshape(expert_count * capacity, width)
    place_gate = (place * gate_of.astype(jnp.bfloat16)[:, None, :]).reshape(place_flat.shape)
    output = (middle + dot_f32(place_gate, returned, 0, 0)).astype(jnp.bfloat16)

    grad_output = cotangent.astype(jnp.float32)
    sign = chosen[0].astype(jnp.float32) - chosen[1].astype(jnp.float32)
    grad_gap = jnp.sum(
        sign * jnp.sum(place.astype(jnp.float32) * grad_gate_slots[:, :, None], axis=1), axis=0
    )
    grad_logits = (sign * (gates[0] * gates[1] * grad_gap)[None, :]).astype(jnp.bfloat16)
    grad_router = dot_f32(norm_two_bf, grad_logits, 0, 1)
    grad_norm_two = dot_f32(
        place_flat, grad_back.reshape(expert_count * capacity, width), 0, 0
    ) + dot_f32(grad_logits, router_full, 0, 1)
    grad_middle, grad_gain_two = rms_pull(middle, inv_two, gain_two, grad_norm_two)
    grad_middle = grad_output + grad_middle
    grad_attn_bf = grad_middle.astype(jnp.bfloat16)
    grad_out_w = dot_f32(attn_bf, grad_attn_bf, 0, 0)
    grad_heads = dot_f32(grad_attn_bf, out_w, 1, 1).astype(jnp.bfloat16)
    grad_q, grad_k, grad_v, tiles = attend_grad(qkv, grad_heads, window, lse)
    grad_qkv = jnp.concatenate([grad_q, grad_k, grad_v], axis=1)
    grad_qkv_w = dot_f32(norm_one_bf, grad_qkv, 0, 0)
    grad_norm_one = dot_f32(grad_qkv, qkv_w, 1, 1)
    grad_tokens, grad_gain_one = rms_pull(inputs, inv_one, gain_one, grad_norm_one)
    grad_tokens = grad_middle + grad_tokens
    grad_table = jnp.einsum(
        "hrc,krc->kh",
        tiles[:, : 2 * TILE],
        one_hot.astype(jnp.float32),
        precision=lax.Precision.HIGHEST,
    )
    far_total = jnp.sum(tiles[:, 2 * TILE :], axis=(1, 2))
    grad_table = grad_table + jnp.where(
        bucket_range[:, None] == buckets - 1, far_total[None, :], 0.0
    )
    table_column = jnp.pad(
        grad_table.reshape(quarters, bias_size), ((0, 0), (0, share - bias_size))
    ).reshape(-1, 1)
    small_grad = jnp.concatenate(
        [grad_router, grad_gain_one[:, None], grad_gain_two[:, None], table_column], axis=1
    )
    small_grad = jnp.pad(small_grad, ((0, 0), (0, small.shape[1] - small_grad.shape[1])))
    dense_grad = jnp.concatenate(
        [
            grad_qkv_w.astype(jnp.bfloat16),
            grad_out_w.astype(jnp.bfloat16),
            small_grad.astype(jnp.bfloat16),
        ],
        axis=1,
    )
    dense_grad = lax.psum_scatter(dense_grad, "dp", scatter_dimension=0, tiled=True)
    dense_grad = lax.psum(dense_grad, ("rep", "expert")).astype(jnp.float32)
    small_sum = dense_grad[:, 4 * width :]
    return (
        output,
        grad_tokens,
        dense_grad[:, :width],
        dense_grad[:, width : 2 * width],
        dense_grad[:, 2 * width : 3 * width],
        dense_grad[:, 3 * width : 4 * width],
        small_sum[:, :expert_count],
        small_sum[:, expert_count],
        small_sum[:, expert_count + 1],
        small_sum[:bias_size, expert_count + 2].reshape(bias_table.shape),
        grad_up.astype(jnp.float32),
        grad_down.astype(jnp.float32),
    )


def solution(mesh):
    placed = (
        P(("rep", "dp", "expert"), None),
        P(("rep", "dp", "expert"), None),
        P(("rep", "dp", "expert"), None),
        P("dp", None),
        P("dp", None),
        P("dp", None),
        P("dp", None),
        P("dp", None),
        P("dp"),
        P("dp"),
        P("dp", None),
        P("expert", None, "dp"),
        P("expert", "dp", None),
    )
    return jax.shard_map(
        local,
        mesh=mesh,
        in_specs=placed,
        out_specs=(
            P(("rep", "dp", "expert"), None),
            P(("rep", "dp", "expert"), None),
            P("dp", None),
            P("dp", None),
            P("dp", None),
            P("dp", None),
            P("dp", None),
            P("dp"),
            P("dp"),
            P("dp", None),
            P("expert", None, "dp"),
            P("expert", "dp", None),
        ),
        check_vma=False,
    )
```
